32 devices in a mesh: dp: 8 (over z, y), fsdp: 4 (over x, core).
Axes of the slice: x: 2, y: 2, z: 4, core: 2. Of those that a mesh axis runs over, the one named last changes fastest.
Arguments:
- picture_tower_inputs: bfloat16 [16384, 1152], P(('dp', 'fsdp')), may hold values from -6 to 6
- caption_tower_inputs: bfloat16 [16384, 1152], P(('dp', 'fsdp')), may hold values from -6 to 6
- halfwidth_parameter_matrix: bfloat16 [1152, 2304], P('fsdp'), may hold values from -0.1875 to 0.1875
- affinity_multiplier: float32 [1], replicated, may hold values from 4 to 12
- affinity_offset: float32 [1], replicated, may hold values from -6 to -2
- precise_parameter_copy: float32 [1152, 2304], P('fsdp', 'dp'), may hold values from -0.125 to 0.125
- gradient_mean_estimate: float32 [1152, 2304], P('fsdp', 'dp'), may hold values from -4 to 4
- gradient_variance_estimate: float32 [1152, 2304], P('fsdp', 'dp'), may hold values from 0.05 to 1
Outputs:
- img_tangent: bfloat16 [16384, 1152], P(('dp', 'fsdp'))
- txt_tangent: bfloat16 [16384, 1152], P(('dp', 'fsdp'))
- new_master: float32 [1152, 2304], P('fsdp', 'dp')
- new_one: float32 [1152, 2304], P('fsdp', 'dp')
- new_two: float32 [1152, 2304], P('fsdp', 'dp')
- new_weights: bfloat16 [1152, 2304], P('fsdp')
The draws below stay inside these ranges and needn't reach their ends.
All inputs are finite; a program needn't handle non-finite values.
Results may differ from the reference program's by a relative error of at most 0.008.
Values may be sent and summed in bfloat16 or wider, within the bound.
A program may use at most 128 MiB of HBM per device.

```python
import math
import jax
import jax.numpy as jnp
from jax import lax

D = 1152
B_DEV = 512
CYCLE = 4
TOKENS = 16384
N_DP = 8
N_FSDP = 4


def level_of(rng, shape, pieces, smallest, high):
    factor_of, own = 1.0, jax.random.fold_in(rng, 6)
    for position, blocks in pieces:
        steps = jnp.exp(jax.random.uniform(jax.random.fold_in(own, position), (blocks,), jnp.float32, smallest / len(pieces), high / len(pieces)))
        factor_of = factor_of * jnp.repeat(steps, shape[position] // blocks).reshape([-1 if axis == position else 1 for axis in range(len(shape))])
    return factor_of


def bell_draw(own_key, shape, width, most, shards=(), held_as=jnp.bfloat16):
    factor_of = level_of(own_key, shape, shards, -0.22, 0.18) if shards else 1.0
    entries = jax.random.normal(own_key, shape, jnp.float32) * width * factor_of
    return jnp.minimum(jnp.maximum(entries, -most), most).astype(held_as)


def setup_inputs(seed: int = 0) -> dict:
    seeds = jax.random.split(jax.random.key(seed), 9)
    return {
        "picture_tower_inputs": bell_draw(seeds[0], (TOKENS, D), 1.0, 6.0, ((0, 32),)),
        "caption_tower_inputs": bell_draw(seeds[1], (TOKENS, D), 1.0, 6.0, ((0, 32),)),
        "halfwidth_parameter_matrix": bell_draw(seeds[2], (D, 2 * D), D ** -0.5, 0.1875, ((0, 4),)),
        "affinity_multiplier": jnp.clip(jnp.exp(jax.random.uniform(seeds[3], (1,), jnp.float32, math.log(4.0), math.log(12.0))), 4.0, 12.0),
        "affinity_offset": jnp.clip(jax.random.uniform(seeds[4], (1,), jnp.float32, -6.0, -2.0), -6.0, -2.0),
        "precise_parameter_copy": bell_draw(seeds[5], (D, 2 * D), 0.008, 0.125, ((0, 4), (1, 8)), jnp.float32),
        "gradient_mean_estimate": bell_draw(seeds[6], (D, 2 * D), 0.3, 4.0, ((0, 4), (1, 8)), jnp.float32),
        "gradient_variance_estimate": jnp.clip(jnp.exp(math.log(1.0) - 2.9957323 * jax.random.uniform(seeds[7], (D, 2 * D), jnp.float32) ** level_of(seeds[7], (D, 2 * D), ((0, 4), (1, 8)), -0.2, 0.2)), 0.05, 1.0),
    }


def normalize(projected):
    inv_norm = lax.rsqrt(lax.optimization_barrier(jnp.sum(projected * projected, axis=-1, keepdims=True)) + 1e-06)
    return (projected * inv_norm, inv_norm)

def reference(picture_tower_inputs, caption_tower_inputs, halfwidth_parameter_matrix, affinity_multiplier, affinity_offset, precise_parameter_copy, gradient_mean_estimate, gradient_variance_estimate):
    proj_img = jnp.dot(picture_tower_inputs, halfwidth_parameter_matrix[:, :D], preferred_element_type=jnp.float32)
    proj_txt = jnp.dot(caption_tower_inputs, halfwidth_parameter_matrix[:, D:], preferred_element_type=jnp.float32)
    unit_img, norm_img = normalize(proj_img)
    normalized_text, norm_txt = normalize(proj_txt)
    low_img = lax.optimization_barrier(unit_img.astype(jnp.bfloat16)).astype(jnp.float32)
    low_txt = lax.optimization_barrier(normalized_text.astype(jnp.bfloat16)).astype(jnp.float32)
    blocks_img = low_img.reshape(N_DP, N_FSDP, B_DEV, D)
    blocks_txt = low_txt.reshape(N_DP, N_FSDP, B_DEV, D)
    affinity_multiplier_name = affinity_multiplier[0]
    shift_value = affinity_offset[0]
    identity_mask = jnp.eye(B_DEV, dtype=jnp.float32)
    grad_img = jnp.zeros_like(blocks_img)
    grad_txt = jnp.zeros_like(blocks_txt)
    for cycle_step in range(CYCLE):
        visiting = jnp.roll(blocks_txt, cycle_step, axis=0)
        logits = affinity_multiplier_name * jnp.einsum('pfid,pfjd->pfij', blocks_img, visiting) + shift_value
        if cycle_step == 0:
            sign_label = 2.0 * identity_mask - 1.0
        else:
            sign_label = -jnp.ones_like(identity_mask)
        pair_weight = (-sign_label * jax.nn.sigmoid(-sign_label * logits) * affinity_multiplier_name).astype(jnp.bfloat16)
        pair_weight = lax.optimization_barrier(pair_weight).astype(jnp.float32)
        grad_img = grad_img + jnp.einsum('pfij,pfjd->pfid', pair_weight, visiting)
        grad_txt = grad_txt + jnp.roll(jnp.einsum('pfij,pfid->pfjd', pair_weight, blocks_img), -cycle_step, axis=0)
    grad_img = grad_img.reshape(TOKENS, D)
    grad_txt = grad_txt.reshape(TOKENS, D)
    img_tangent = (norm_img * (grad_img - unit_img * lax.optimization_barrier(jnp.sum(unit_img * grad_img, axis=1, keepdims=True)))).astype(jnp.bfloat16)
    txt_tangent = (norm_txt * (grad_txt - normalized_text * lax.optimization_barrier(jnp.sum(normalized_text * grad_txt, axis=1, keepdims=True)))).astype(jnp.bfloat16)
    gradient = jnp.concatenate([jnp.dot(picture_tower_inputs.T, img_tangent, preferred_element_type=jnp.float32), jnp.dot(caption_tower_inputs.T, txt_tangent, preferred_element_type=jnp.float32)], axis=1)
    new_one = 0.9 * gradient_mean_estimate + 0.1 * gradient
    new_two = 0.95 * gradient_variance_estimate + 0.05 * gradient * gradient
    new_master = precise_parameter_copy - 0.001 * (new_one / (jnp.sqrt(new_two) + 1e-08) + 0.1 * precise_parameter_copy)
    return (img_tangent, txt_tangent, new_master, new_one, new_two, new_master.astype(jnp.bfloat16))
```

```python
import jax
import jax.numpy as jnp
from jax import lax
from jax.sharding import PartitionSpec as P

CYCLE = 4


def shifted(value, axis, steps):
    count = lax.axis_size(axis)
    pairs = [(source, (source + steps) % count) for source in range(count)]
    return lax.ppermute(value, axis, pairs)


def swapped(value, axis, bit):
    count = lax.axis_size(axis)
    return lax.ppermute(value, axis, [(source, source ^ bit) for source in range(count)])


def bit_of(axis, bit):
    return (lax.axis_index(axis) // bit) % 2 == 1


def ordered(mine, other, high):
    return jnp.where(high, other, mine), jnp.where(high, mine, other)


def normalize(projected):
    inv_norm = lax.rsqrt(jnp.sum(projected * projected, axis=-1, keepdims=True) + 1e-06)
    return (projected * inv_norm, inv_norm)


def contract_rows(left, right):
    return lax.dot_general(
        left, right, (((0,), (0,)), ((), ())), preferred_element_type=jnp.float32
    )


def weigh_pairs(left, right, scale, shift, sign_label):
    logits = (
        scale
        * lax.dot_general(
            left, right, (((1,), (1,)), ((), ())), preferred_element_type=jnp.float32
        )
        + shift
    )
    return (-sign_label * jax.nn.sigmoid(-sign_label * logits) * scale).astype(jnp.bfloat16)


def gather_weights(shard):
    rows = shard.shape[0]
    half = rows // 2
    y = bit_of("dp", 1)
    x = bit_of("fsdp", 2)
    c = bit_of("fsdp", 1)
    mine = jnp.where(y, shard[half:], shard[:half])
    got = swapped(mine, "fsdp", 2)
    rest = swapped(got, "dp", 1)
    low, high = ordered(got, rest, y)
    remote = jnp.concatenate([low, high], axis=0)
    own_core = swapped(shard, "fsdp", 1)
    remote_core = swapped(remote, "fsdp", 1)
    own_pair = jnp.concatenate(ordered(shard, own_core, c), axis=0)
    remote_pair = jnp.concatenate(ordered(remote, remote_core, c), axis=0)
    return jnp.concatenate(ordered(own_pair, remote_pair, x), axis=0)


def tangent(inv_norm, unit, grad):
    return (inv_norm * (grad - unit * jnp.sum(unit * grad, axis=1, keepdims=True))).astype(
        jnp.bfloat16
    )


def reduce_half(value, dim, axis, bit):
    high = bit_of(axis, bit)
    low_half = lax.index_in_dim(value, 0, dim, keepdims=False)
    high_half = lax.index_in_dim(value, 1, dim, keepdims=False)
    send = jnp.where(high, low_half, high_half).astype(jnp.bfloat16)
    keep = jnp.where(high, high_half, low_half).astype(jnp.float32)
    return keep + swapped(send, axis, bit).astype(jnp.float32)


def body(
    picture_tower_inputs,
    caption_tower_inputs,
    halfwidth_parameter_matrix,
    affinity_multiplier,
    affinity_offset,
    precise_parameter_copy,
    gradient_mean_estimate,
    gradient_variance_estimate,
):
    row_count, width = picture_tower_inputs.shape
    n_dp = lax.axis_size("dp")
    scale = affinity_multiplier[0]
    shift = affinity_offset[0]

    weights_img = gather_weights(halfwidth_parameter_matrix[:, :width])
    weights_txt = gather_weights(halfwidth_parameter_matrix[:, width:])
    unit_img, norm_img = normalize(
        jnp.dot(picture_tower_inputs, weights_img, preferred_element_type=jnp.float32)
    )
    unit_txt, norm_txt = normalize(
        jnp.dot(caption_tower_inputs, weights_txt, preferred_element_type=jnp.float32)
    )
    low_img = unit_img.astype(jnp.bfloat16)
    low_txt = unit_txt.astype(jnp.bfloat16)

    diagonal = 2.0 * jnp.eye(row_count, dtype=jnp.float32) - 1.0
    pair_weight = weigh_pairs(low_img, low_txt, scale, shift, diagonal)
    grad_img = jnp.dot(pair_weight, low_txt, preferred_element_type=jnp.float32)
    grad_txt = contract_rows(pair_weight, low_img)
    visiting_txt, visiting_img = low_txt, low_img
    for _ in range(1, CYCLE):
        visiting_img = shifted(visiting_img, "dp", -1)
        visiting_txt = shifted(visiting_txt, "dp", 1)
        of_img = weigh_pairs(low_img, visiting_txt, scale, shift, -1.0)
        of_txt = weigh_pairs(low_txt, visiting_img, scale, shift, -1.0)
        grad_img = grad_img + jnp.dot(of_img, visiting_txt, preferred_element_type=jnp.float32)
        grad_txt = grad_txt + jnp.dot(of_txt, visiting_img, preferred_element_type=jnp.float32)
    img_tangent = tangent(norm_img, unit_img, grad_img)
    txt_tangent = tangent(norm_txt, unit_txt, grad_txt)

    owned = 2 * width // n_dp
    piece = width // 2
    pieces = []
    for y in range(2):
        for features, rows in (
            (picture_tower_inputs, img_tangent),
            (caption_tower_inputs, txt_tangent),
        ):
            columns = rows.reshape(row_count, n_dp // 4, 2, owned)[:, :, y].reshape(row_count, piece)
            pieces.append(contract_rows(features, columns).astype(jnp.bfloat16))
    shard_rows = width // lax.axis_size("fsdp")
    half = shard_rows // 2
    split = [p.reshape(2, 2, 2, half, piece) for p in pieces]

    new_parts = []
    for part in range(2):
        total = jnp.stack([s[:, :, part] for s in split]).reshape(2, 2, 2, 2, half, piece)
        total = reduce_half(total, 3, "fsdp", 1)
        if part == 0:
            total = reduce_half(total, 2, "fsdp", 2)
            total = reduce_half(total, 0, "dp", 1)
        else:
            total = reduce_half(total, 0, "dp", 1)
            total = reduce_half(total, 1, "fsdp", 2)
        total = reduce_half(total, 0, "dp", n_dp // 2)
        bit = n_dp // 4
        while bit > 1:
            size = total.shape[-1] // 2
            total = reduce_half(jnp.stack([total[:, :size], total[:, size:]]), 0, "dp", bit)
            bit //= 2
        rows = slice(part * half, (part + 1) * half)
        new_one = 0.9 * gradient_mean_estimate[rows] + 0.1 * total
        new_two = 0.95 * gradient_variance_estimate[rows] + 0.05 * total * total
        master = precise_parameter_copy[rows]
        new_master = master - 0.001 * (new_one / (jnp.sqrt(new_two) + 1e-08) + 0.1 * master)

        gathered = new_master.astype(jnp.bfloat16)[None]
        bit = n_dp // 2
        order = []
        while bit >= 1:
            other = swapped(gathered, "dp", bit)
            gathered = jnp.concatenate(ordered(gathered, other, bit_of("dp", bit)), axis=0)
            order.append(bit)
            bit //= 2
        bits = len(order)
        gathered = gathered.reshape((2,) * bits + (half, owned))
        gathered = gathered.transpose((bits,) + tuple(reversed(range(bits))) + (bits + 1,))
        new_parts.append((new_master, new_one, new_two, gathered.reshape(half, 2 * width)))
    new_master, new_one, new_two, new_weights = (
        jnp.concatenate(both, axis=0) for both in zip(*new_parts)
    )
    return (img_tangent, txt_tangent, new_master, new_one, new_two, new_weights)


def solution(mesh):
    return jax.shard_map(
        body,
        mesh=mesh,
        in_specs=(
            P(("dp", "fsdp"), None),
            P(("dp", "fsdp"), None),
            P("fsdp", None),
            P(),
            P(),
            P("fsdp", "dp"),
            P("fsdp", "dp"),
            P("fsdp", "dp"),
        ),
        out_specs=(
            P(("dp", "fsdp"), None),
            P(("dp", "fsdp"), None),
            P("fsdp", "dp"),
            P("fsdp", "dp"),
            P("fsdp", "dp"),
            P("fsdp", None),
        ),
        check_vma=False,
    )
```

```python
import jax
import jax.numpy as jnp
from jax import lax
from jax.sharding import PartitionSpec as P

CYCLE = 4


def shifted(value, axis, steps):
    count = lax.axis_size(axis)
    pairs = [(source, (source + steps) % count) for source in range(count)]
    return lax.ppermute(value, axis, pairs)


def swapped(value, axis, bit):
    count = lax.axis_size(axis)
    return lax.ppermute(value, axis, [(source, source ^ bit) for source in range(count)])


def bit_of(axis, bit):
    return (lax.axis_index(axis) // bit) % 2 == 1


def ordered(mine, other, high):
    return jnp.where(high, other, mine), jnp.where(high, mine, other)


def normalize(projected):
    inv_norm = lax.rsqrt(jnp.sum(projected * projected, axis=-1, keepdims=True) + 1e-06)
    return (projected * inv_norm, inv_norm)


def contract_rows(left, right):
    return lax.dot_general(
        left, right, (((0,), (0,)), ((), ())), preferred_element_type=jnp.float32
    )


def weigh_pairs(left, right, scale, shift, sign_label):
    logits = (
        scale
        * lax.dot_general(
            left, right, (((1,), (1,)), ((), ())), preferred_element_type=jnp.float32
        )
        + shift
    )
    return (-sign_label * jax.nn.sigmoid(-sign_label * logits) * scale).astype(jnp.bfloat16)


def gather_weights(shard):
    rows = shard.shape[0]
    half = rows // 2
    y = bit_of("dp", 1)
    x = bit_of("fsdp", 2)
    c = bit_of("fsdp", 1)
    mine = jnp.where(y, shard[half:], shard[:half])
    got = swapped(mine, "fsdp", 2)
    rest = swapped(got, "dp", 1)
    low, high = ordered(got, rest, y)
    remote = jnp.concatenate([low, high], axis=0)
    own_core = swapped(shard, "fsdp", 1)
    remote_core = swapped(remote, "fsdp", 1)
    own_pair = jnp.concatenate(ordered(shard, own_core, c), axis=0)
    remote_pair = jnp.concatenate(ordered(remote, remote_core, c), axis=0)
    return jnp.concatenate(ordered(own_pair, remote_pair, x), axis=0)


def tangent(inv_norm, unit, grad):
    return (inv_norm * (grad - unit * jnp.sum(unit * grad, axis=1, keepdims=True))).astype(
        jnp.bfloat16
    )


def reduce_half(value, dim, axis, bit):
    high = bit_of(axis, bit)
    low_half = lax.index_in_dim(value, 0, dim, keepdims=False)
    high_half = lax.index_in_dim(value, 1, dim, keepdims=False)
    send = jnp.where(high, low_half, high_half).astype(jnp.bfloat16)
    keep = jnp.where(high, high_half, low_half).astype(jnp.float32)
    return keep + swapped(send, axis, bit).astype(jnp.float32)


def body(
    picture_tower_inputs,
    caption_tower_inputs,
    halfwidth_parameter_matrix,
    affinity_multiplier,
    affinity_offset,
    precise_parameter_copy,
    gradient_mean_estimate,
    gradient_variance_estimate,
):
    row_count, width = picture_tower_inputs.shape
    n_dp = lax.axis_size("dp")
    scale = affinity_multiplier[0]
    shift = affinity_offset[0]

    weights_img = gather_weights(halfwidth_parameter_matrix[:, :width])
    weights_txt = gather_weights(halfwidth_parameter_matrix[:, width:])
    unit_img, norm_img = normalize(
        jnp.dot(picture_tower_inputs, weights_img, preferred_element_type=jnp.float32)
    )
    unit_txt, norm_txt = normalize(
        jnp.dot(caption_tower_inputs, weights_txt, preferred_element_type=jnp.float32)
    )
    low_img = unit_img.astype(jnp.bfloat16)
    low_txt = unit_txt.astype(jnp.bfloat16)

    y = bit_of("dp", 1)
    cuts = 2
    size = row_count // cuts
    across = swapped(jnp.where(y, low_img, low_txt), "dp", 1)
    txt_behind = [shifted(low_txt[i * size : (i + 1) * size], "dp", 2) for i in range(cuts)]
    img_ahead = [shifted(low_img[i * size : (i + 1) * size], "dp", -2) for i in range(cuts)]
    txt_beside = [swapped(v, "dp", 1) for v in txt_behind]
    img_beside = [swapped(v, "dp", 1) for v in img_ahead]
    onward = [(s, (s + (2 if s % 2 == 0 else -2)) % n_dp) for s in range(n_dp)]
    last = [
        lax.ppermute(jnp.where(y, i, t), "dp", onward) for t, i in zip(txt_beside, img_beside)
    ]

    def met(own, block, sign_label=-1.0):
        pair_weight = lax.optimization_barrier(weigh_pairs(own, block, scale, shift, sign_label))
        return pair_weight, jnp.dot(pair_weight, block, preferred_element_type=jnp.float32)

    diagonal = 2.0 * jnp.eye(row_count, dtype=jnp.float32) - 1.0
    pair_weight, grad_img = met(low_img, low_txt, diagonal)
    grad_txt = contract_rows(pair_weight, low_img)
    of_across = met(jnp.where(y, low_img, low_txt), across)[1]
    grad_img = grad_img + jnp.where(y, of_across, 0.0)
    grad_txt = grad_txt + jnp.where(y, 0.0, of_across)
    for t, i in zip(txt_behind + txt_beside, img_ahead + img_beside):
        grad_img = grad_img + met(low_img, t)[1]
        grad_txt = grad_txt + met(low_txt, i)[1]
    own_last = jnp.where(y, low_txt, low_img)
    of_last = sum(met(own_last, v)[1] for v in last)
    grad_img = grad_img + jnp.where(y, 0.0, of_last)
    grad_txt = grad_txt + jnp.where(y, of_last, 0.0)
    img_tangent = tangent(norm_img, unit_img, grad_img)
    txt_tangent = tangent(norm_txt, unit_txt, grad_txt)

    owned = 2 * width // n_dp
    piece = width // 2
    pieces = []
    for y in range(2):
        for features, rows in (
            (picture_tower_inputs, img_tangent),
            (caption_tower_inputs, txt_tangent),
        ):
            columns = rows.reshape(row_count, n_dp // 4, 2, owned)[:, :, y].reshape(row_count, piece)
            pieces.append(contract_rows(features, columns).astype(jnp.bfloat16))
    shard_rows = width // lax.axis_size("fsdp")
    half = shard_rows // 2
    split = [p.reshape(2, 2, 2, half, piece) for p in pieces]

    new_parts = []
    for part in range(2):
        total = jnp.stack([s[:, :, part] for s in split]).reshape(2, 2, 2, 2, half, piece)
        total = reduce_half(total, 3, "fsdp", 1)
        if part == 0:
            total = reduce_half(total, 2, "fsdp", 2)
            total = reduce_half(total, 0, "dp", 1)
        else:
            total = reduce_half(total, 0, "dp", 1)
            total = reduce_half(total, 1, "fsdp", 2)
        total = reduce_half(total, 0, "dp", n_dp // 2)
        bit = n_dp // 4
        while bit > 1:
            size = total.shape[-1] // 2
            total = reduce_half(jnp.stack([total[:, :size], total[:, size:]]), 0, "dp", bit)
            bit //= 2
        rows = slice(part * half, (part + 1) * half)
        new_one = 0.9 * gradient_mean_estimate[rows] + 0.1 * total
        new_two = 0.95 * gradient_variance_estimate[rows] + 0.05 * total * total
        master = precise_parameter_copy[rows]
        new_master = master - 0.001 * (new_one / (jnp.sqrt(new_two) + 1e-08) + 0.1 * master)

        gathered = new_master.astype(jnp.bfloat16)[None]
        bit = n_dp // 2
        order = []
        while bit >= 1:
            other = swapped(gathered, "dp", bit)
            gathered = jnp.concatenate(ordered(gathered, other, bit_of("dp", bit)), axis=0)
            order.append(bit)
            bit //= 2
        bits = len(order)
        gathered = gathered.reshape((2,) * bits + (half, owned))
        gathered = gathered.transpose((bits,) + tuple(reversed(range(bits))) + (bits + 1,))
        new_parts.append((new_master, new_one, new_two, gathered.reshape(half, 2 * width)))
    new_master, new_one, new_two, new_weights = (
        jnp.concatenate(both, axis=0) for both in zip(*new_parts)
    )
    return (img_tangent, txt_tangent, new_master, new_one, new_two, new_weights)


def solution(mesh):
    return jax.shard_map(
        body,
        mesh=mesh,
        in_specs=(
            P(("dp", "fsdp"), None),
            P(("dp", "fsdp"), None),
            P("fsdp", None),
            P(),
            P(),
            P("fsdp", "dp"),
            P("fsdp", "dp"),
            P("fsdp", "dp"),
        ),
        out_specs=(
            P(("dp", "fsdp"), None),
            P(("dp", "fsdp"), None),
            P("fsdp", "dp"),
            P("fsdp", "dp"),
            P("fsdp", "dp"),
            P("fsdp", None),
        ),
        check_vma=False,
    )
```

```python
import jax
import jax.numpy as jnp
from jax import lax
from jax.experimental import pallas as pl
from jax.experimental.pallas import tpu as pltpu
from jax.sharding import PartitionSpec as P

CYCLE = 4


def shifted(value, axis, steps):
    count = lax.axis_size(axis)
    pairs = [(source, (source + steps) % count) for source in range(count)]
    return lax.ppermute(value, axis, pairs)


def swapped(value, axis, bit):
    count = lax.axis_size(axis)
    return lax.ppermute(value, axis, [(source, source ^ bit) for source in range(count)])


def bit_of(axis, bit):
    return (lax.axis_index(axis) // bit) % 2 == 1


def ordered(mine, other, high):
    return jnp.where(high, other, mine), jnp.where(high, mine, other)


def normalize(projected):
    inv_norm = lax.rsqrt(jnp.sum(projected * projected, axis=-1, keepdims=True) + 1e-06)
    return (projected * inv_norm, inv_norm)


def contract_rows(left, right):
    return lax.dot_general(
        left, right, (((0,), (0,)), ((), ())), preferred_element_type=jnp.float32
    )


def weigh_pairs(left, right, scale, shift, sign_label):
    logits = (
        scale
        * lax.dot_general(
            left, right, (((1,), (1,)), ((), ())), preferred_element_type=jnp.float32
        )
        + shift
    )
    return (-sign_label * jax.nn.sigmoid(-sign_label * logits) * scale).astype(jnp.bfloat16)


def gather_weights(shard):
    rows = shard.shape[0]
    half = rows // 2
    y = bit_of("dp", 1)
    x = bit_of("fsdp", 2)
    c = bit_of("fsdp", 1)
    mine = jnp.where(y, shard[half:], shard[:half])
    got = swapped(mine, "fsdp", 2)
    rest = swapped(got, "dp", 1)
    low, high = ordered(got, rest, y)
    remote = jnp.concatenate([low, high], axis=0)
    own_core = swapped(shard, "fsdp", 1)
    remote_core = swapped(remote, "fsdp", 1)
    own_pair = jnp.concatenate(ordered(shard, own_core, c), axis=0)
    remote_pair = jnp.concatenate(ordered(remote, remote_core, c), axis=0)
    return jnp.concatenate(ordered(own_pair, remote_pair, x), axis=0)


def tangent(inv_norm, unit, grad):
    return (inv_norm * (grad - unit * jnp.sum(unit * grad, axis=1, keepdims=True))).astype(
        jnp.bfloat16
    )


def gradient_kernel(img_ref, txt_ref, img_tan_ref, txt_tan_ref, order_ref, out_ref, columns_ref):
    row_count, width = img_ref.shape
    piece = out_ref.shape[-1]
    padded = columns_ref.shape[-1] // 2
    step = 384 if width % 384 == 0 else 128
    for tower, (features, rows) in enumerate(((img_ref, img_tan_ref), (txt_ref, txt_tan_ref))):
        for start in range(0, row_count, 256):
            chunk = slice(start, start + 256)
            columns_ref[chunk, :] = jnp.dot(
                rows[chunk, :], order_ref[...], preferred_element_type=jnp.float32
            ).astype(jnp.bfloat16)

        @pl.loop(0, width // step)
        def _(block):
            at = pl.multiple_of(block * step, step)
            left = features[:, pl.ds(at, step)]
            for y in range(2):
                right = columns_ref[:, y * padded : y * padded + piece]
                out_ref[y, tower, pl.ds(at, step), :] = contract_rows(left, right).astype(
                    jnp.bfloat16
                )


def weight_gradient(img, txt, img_tangent, txt_tangent, n_dp, owned):
    row_count, width = img.shape
    piece = width // 2
    padded = -(-piece // 128) * 128
    source = jnp.arange(width)
    block = source // owned
    target = (block % 2) * padded + (block // 2) * owned + source % owned
    order = (target[:, None] == jnp.arange(2 * padded)[None, :]).astype(jnp.bfloat16)
    out = pl.pallas_call(
        gradient_kernel,
        out_shape=jax.ShapeDtypeStruct((2, 2, width, piece), jnp.bfloat16),
        in_specs=[pl.BlockSpec(memory_space=pltpu.VMEM)] * 5,
        out_specs=pl.BlockSpec(memory_space=pltpu.VMEM),
        scratch_shapes=[pltpu.VMEM((row_count, 2 * padded), jnp.bfloat16)],
        compiler_params=pltpu.CompilerParams(vmem_limit_bytes=32 * 2**20),
    )(img, txt, img_tangent, txt_tangent, order)
    return [out[y, tower] for y in range(2) for tower in range(2)]


def reduce_half(value, dim, axis, bit):
    high = bit_of(axis, bit)
    low_half = lax.index_in_dim(value, 0, dim, keepdims=False)
    high_half = lax.index_in_dim(value, 1, dim, keepdims=False)
    send = jnp.where(high, low_half, high_half).astype(jnp.bfloat16)
    keep = jnp.where(high, high_half, low_half).astype(jnp.float32)
    return keep + swapped(send, axis, bit).astype(jnp.float32)


def body(
    picture_tower_inputs,
    caption_tower_inputs,
    halfwidth_parameter_matrix,
    affinity_multiplier,
    affinity_offset,
    precise_parameter_copy,
    gradient_mean_estimate,
    gradient_variance_estimate,
):
    row_count, width = picture_tower_inputs.shape
    n_dp = lax.axis_size("dp")
    scale = affinity_multiplier[0]
    shift = affinity_offset[0]

    weights_img = gather_weights(halfwidth_parameter_matrix[:, :width])
    weights_txt = gather_weights(halfwidth_parameter_matrix[:, width:])
    unit_img, norm_img = normalize(
        jnp.dot(picture_tower_inputs, weights_img, preferred_element_type=jnp.float32)
    )
    unit_txt, norm_txt = normalize(
        jnp.dot(caption_tower_inputs, weights_txt, preferred_element_type=jnp.float32)
    )
    low_img = unit_img.astype(jnp.bfloat16)
    low_txt = unit_txt.astype(jnp.bfloat16)

    y = bit_of("dp", 1)
    cuts = 2
    size = row_count // cuts
    own_across = jnp.where(y, low_img, low_txt)
    across = [swapped(own_across[:size], "dp", 1)]
    txt_behind, img_ahead = [], []
    for i in range(cuts):
        txt_behind.append(shifted(low_txt[i * size : (i + 1) * size], "dp", 2))
        img_ahead.append(shifted(low_img[i * size : (i + 1) * size], "dp", -2))
    onward = [(s, (s + (2 if s % 2 == 0 else -2)) % n_dp) for s in range(n_dp)]
    txt_beside, img_beside, last = [], [], []
    before = across[0]
    for i in range(cuts):
        txt_behind[i], before = lax.optimization_barrier((txt_behind[i], before))
        if i == 0:
            across[0] = before
        else:
            img_beside[i - 1] = before
        beside = swapped(txt_behind[i], "dp", 1)
        if i > 0:
            last.append(lax.ppermute(jnp.where(y, img_beside[i - 1], txt_beside[i - 1]), "dp", onward))
        img_ahead[i], beside = lax.optimization_barrier((img_ahead[i], beside))
        txt_beside.append(beside)
        before = swapped(img_ahead[i], "dp", 1)
        img_beside.append(before)
    rest, img_beside[-1] = lax.optimization_barrier((own_across[size:], img_beside[-1]))
    across.append(swapped(rest, "dp", 1))
    last.append(lax.ppermute(jnp.where(y, img_beside[-1], txt_beside[-1]), "dp", onward))

    def met(own, block, sign_label=-1.0):
        pair_weight = lax.optimization_barrier(weigh_pairs(own, block, scale, shift, sign_label))
        return pair_weight, jnp.dot(pair_weight, block, preferred_element_type=jnp.float32)

    diagonal = 2.0 * jnp.eye(row_count, dtype=jnp.float32) - 1.0
    pair_weight, grad_img = met(low_img, low_txt, diagonal)
    grad_txt = contract_rows(pair_weight, low_img)
    of_across = sum(met(own_across, v)[1] for v in across)
    grad_img = grad_img + jnp.where(y, of_across, 0.0)
    grad_txt = grad_txt + jnp.where(y, 0.0, of_across)
    for t, i in zip(txt_behind + txt_beside, img_ahead + img_beside):
        grad_img = grad_img + met(low_img, t)[1]
        grad_txt = grad_txt + met(low_txt, i)[1]
    own_last = jnp.where(y, low_txt, low_img)
    of_last = sum(met(own_last, v)[1] for v in last)
    grad_img = grad_img + jnp.where(y, 0.0, of_last)
    grad_txt = grad_txt + jnp.where(y, of_last, 0.0)
    img_tangent = tangent(norm_img, unit_img, grad_img)
    txt_tangent = tangent(norm_txt, unit_txt, grad_txt)

    owned = 2 * width // n_dp
    piece = width // 2
    pieces = weight_gradient(
        picture_tower_inputs, caption_tower_inputs, img_tangent, txt_tangent, n_dp, owned
    )
    shard_rows = width // lax.axis_size("fsdp")
    half = shard_rows // 2
    split = [p.reshape(2, 2, 2, half, piece) for p in pieces]

    new_parts = []
    for part in range(2):
        total = jnp.stack([s[:, :, part] for s in split]).reshape(2, 2, 2, 2, half, piece)
        total = reduce_half(total, 3, "fsdp", 1)
        if part == 0:
            total = reduce_half(total, 2, "fsdp", 2)
            total = reduce_half(total, 0, "dp", 1)
        else:
            total = reduce_half(total, 0, "dp", 1)
            total = reduce_half(total, 1, "fsdp", 2)
        total = reduce_half(total, 0, "dp", n_dp // 2)
        bit = n_dp // 4
        while bit > 1:
            size = total.shape[-1] // 2
            total = reduce_half(jnp.stack([total[:, :size], total[:, size:]]), 0, "dp", bit)
            bit //= 2
        rows = slice(part * half, (part + 1) * half)
        new_one = 0.9 * gradient_mean_estimate[rows] + 0.1 * total
        new_two = 0.95 * gradient_variance_estimate[rows] + 0.05 * total * total
        master = precise_parameter_copy[rows]
        new_master = master - 0.001 * (new_one / (jnp.sqrt(new_two) + 1e-08) + 0.1 * master)

        gathered = new_master.astype(jnp.bfloat16)[None]
        bit = n_dp // 2
        order = []
        while bit >= 1:
            other = swapped(gathered, "dp", bit)
            gathered = jnp.concatenate(ordered(gathered, other, bit_of("dp", bit)), axis=0)
            order.append(bit)
            bit //= 2
        bits = len(order)
        gathered = gathered.reshape((2,) * bits + (half, owned))
        gathered = gathered.transpose((bits,) + tuple(reversed(range(bits))) + (bits + 1,))
        new_parts.append((new_master, new_one, new_two, gathered.reshape(half, 2 * width)))
    new_master, new_one, new_two, new_weights = (
        jnp.concatenate(both, axis=0) for both in zip(*new_parts)
    )
    return (img_tangent, txt_tangent, new_master, new_one, new_two, new_weights)


def solution(mesh):
    return jax.shard_map(
        body,
        mesh=mesh,
        in_specs=(
            P(("dp", "fsdp"), None),
            P(("dp", "fsdp"), None),
            P("fsdp", None),
            P(),
            P(),
            P("fsdp", "dp"),
            P("fsdp", "dp"),
            P("fsdp", "dp"),
        ),
        out_specs=(
            P(("dp", "fsdp"), None),
            P(("dp", "fsdp"), None),
            P("fsdp", "dp"),
            P("fsdp", "dp"),
            P("fsdp", "dp"),
            P("fsdp", None),
        ),
        check_vma=False,
    )
```

```python
import jax
import jax.numpy as jnp
from jax import lax
from jax.experimental import pallas as pl
from jax.experimental.pallas import tpu as pltpu
from jax.sharding import PartitionSpec as P

CYCLE = 4


def shifted(value, axis, steps):
    count = lax.axis_size(axis)
    pairs = [(source, (source + steps) % count) for source in range(count)]
    return lax.ppermute(value, axis, pairs)


def swapped(value, axis, bit):
    count = lax.axis_size(axis)
    return lax.ppermute(value, axis, [(source, source ^ bit) for source in range(count)])


def bit_of(axis, bit):
    return (lax.axis_index(axis) // bit) % 2 == 1


def ordered(mine, other, high):
    return jnp.where(high, other, mine), jnp.where(high, mine, other)


def project_kernel(rows_ref, weights_ref, unit_ref, low_ref, norm_ref):
    step = 128

    @pl.loop(0, rows_ref.shape[0] // step)
    def _(block):
        at = pl.ds(pl.multiple_of(block * step, step), step)
        projected = jnp.dot(
            rows_ref[at, :], weights_ref[...], preferred_element_type=jnp.float32
        )
        inv_norm = lax.rsqrt(jnp.sum(projected * projected, axis=-1, keepdims=True) + 1e-06)
        unit = projected * inv_norm
        unit_ref[at, :] = unit
        low_ref[at, :] = unit.astype(jnp.bfloat16)
        norm_ref[at, :] = inv_norm


def project(rows, weights):
    shape = (rows.shape[0], weights.shape[1])
    return pl.pallas_call(
        project_kernel,
        out_shape=(
            jax.ShapeDtypeStruct(shape, jnp.float32),
            jax.ShapeDtypeStruct(shape, jnp.bfloat16),
            jax.ShapeDtypeStruct((shape[0], 1), jnp.float32),
        ),
        in_specs=[pl.BlockSpec(memory_space=pltpu.VMEM)] * 2,
        out_specs=[pl.BlockSpec(memory_space=pltpu.VMEM)] * 3,
        compiler_params=pltpu.CompilerParams(vmem_limit_bytes=32 * 2**20),
    )(rows, weights)


def gather_kernel(own_ref, out_ref, z_send, z_recv, y_send, y_recv):
    n = out_ref.shape[0]
    steps = n // 2
    me = lax.axis_index("dp")
    after = lax.rem(me + 2, n)
    before = lax.rem(me + n - 2, n)
    beside = me + 1 - 2 * lax.rem(me, 2)
    barrier = pltpu.get_barrier_semaphore()
    for other in (after, before, beside):
        pl.semaphore_signal(
            barrier, inc=1, device_id={"dp": other}, device_id_type=pl.DeviceIdType.MESH
        )
    pl.semaphore_wait(barrier, 3)
    out_ref[me] = own_ref[...]
    along, across = [], []
    for step in range(steps):
        block = lax.rem(me - 2 * step + 2 * n, n)
        if step > 0:
            along[step - 1].wait_recv()
        for copies, target, sends, receives in (
            (along, after, z_send, z_recv),
            (across, beside, y_send, y_recv),
        ):
            if copies is along and step == steps - 1:
                continue
            copy = pltpu.make_async_remote_copy(
                src_ref=out_ref.at[block],
                dst_ref=out_ref.at[block],
                send_sem=sends.at[step],
                recv_sem=receives.at[step],
                device_id={"dp": target},
                device_id_type=pl.DeviceIdType.MESH,
            )
            copy.start()
            copies.append(copy)
    for copy in along:
        copy.wait_send()
    for copy in across:
        copy.wait()


def gather_columns(own, n_dp):
    return pl.pallas_call(
        gather_kernel,
        out_shape=jax.ShapeDtypeStruct((n_dp,) + own.shape, own.dtype),
        in_specs=[pl.BlockSpec(memory_space=pltpu.VMEM)],
        out_specs=pl.BlockSpec(memory_space=pltpu.VMEM),
        scratch_shapes=[pltpu.SemaphoreType.DMA((n_dp // 2,))] * 4,
        compiler_params=pltpu.CompilerParams(
            collective_id=0, has_side_effects=True, vmem_limit_bytes=32 * 2**20
        ),
    )(own)


def contract_rows(left, right):
    return lax.dot_general(
        left, right, (((0,), (0,)), ((), ())), preferred_element_type=jnp.float32
    )


def weigh_pairs(left, right, scale, shift, sign_label):
    logits = (
        scale
        * lax.dot_general(
            left, right, (((1,), (1,)), ((), ())), preferred_element_type=jnp.float32
        )
        + shift
    )
    return (-sign_label * jax.nn.sigmoid(-sign_label * logits) * scale).astype(jnp.bfloat16)


def gather_weights(shard):
    rows = shard.shape[0]
    half = rows // 2
    y = bit_of("dp", 1)
    x = bit_of("fsdp", 2)
    c = bit_of("fsdp", 1)
    mine = jnp.where(y, shard[half:], shard[:half])
    got = swapped(mine, "fsdp", 2)
    rest = swapped(got, "dp", 1)
    low, high = ordered(got, rest, y)
    remote = jnp.concatenate([low, high], axis=0)
    own_core = swapped(shard, "fsdp", 1)
    remote_core = swapped(remote, "fsdp", 1)
    own_pair = jnp.concatenate(ordered(shard, own_core, c), axis=0)
    remote_pair = jnp.concatenate(ordered(remote, remote_core, c), axis=0)
    return jnp.concatenate(ordered(own_pair, remote_pair, x), axis=0)


def tangent(inv_norm, unit, grad):
    return (inv_norm * (grad - unit * jnp.sum(unit * grad, axis=1, keepdims=True))).astype(
        jnp.bfloat16
    )


def gradient_kernel(img_ref, txt_ref, img_tan_ref, txt_tan_ref, order_ref, out_ref, columns_ref):
    row_count, width = img_ref.shape
    piece = out_ref.shape[-1]
    padded = columns_ref.shape[-1] // 2
    step = 384 if width % 384 == 0 else 128
    for tower, (features, rows) in enumerate(((img_ref, img_tan_ref), (txt_ref, txt_tan_ref))):
        for start in range(0, row_count, 256):
            chunk = slice(start, start + 256)
            columns_ref[chunk, :] = jnp.dot(
                rows[chunk, :], order_ref[...], preferred_element_type=jnp.float32
            ).astype(jnp.bfloat16)

        @pl.loop(0, width // step)
        def _(block):
            at = pl.multiple_of(block * step, step)
            left = features[:, pl.ds(at, step)]
            for y in range(2):
                right = columns_ref[:, y * padded : y * padded + piece]
                out_ref[y, tower, pl.ds(at, step), :] = contract_rows(left, right).astype(
                    jnp.bfloat16
                )


def weight_gradient(img, txt, img_tangent, txt_tangent, n_dp, owned):
    row_count, width = img.shape
    piece = width // 2
    padded = -(-piece // 128) * 128
    source = jnp.arange(width)
    block = source // owned
    target = (block % 2) * padded + (block // 2) * owned + source % owned
    order = (target[:, None] == jnp.arange(2 * padded)[None, :]).astype(jnp.bfloat16)
    out = pl.pallas_call(
        gradient_kernel,
        out_shape=jax.ShapeDtypeStruct((2, 2, width, piece), jnp.bfloat16),
        in_specs=[pl.BlockSpec(memory_space=pltpu.VMEM)] * 5,
        out_specs=pl.BlockSpec(memory_space=pltpu.VMEM),
        scratch_shapes=[pltpu.VMEM((row_count, 2 * padded), jnp.bfloat16)],
        compiler_params=pltpu.CompilerParams(vmem_limit_bytes=32 * 2**20),
    )(img, txt, img_tangent, txt_tangent, order)
    return [out[y, tower] for y in range(2) for tower in range(2)]


def reduce_half(value, dim, axis, bit):
    high = bit_of(axis, bit)
    low_half = lax.index_in_dim(value, 0, dim, keepdims=False)
    high_half = lax.index_in_dim(value, 1, dim, keepdims=False)
    send = jnp.where(high, low_half, high_half).astype(jnp.bfloat16)
    keep = jnp.where(high, high_half, low_half).astype(jnp.float32)
    return keep + swapped(send, axis, bit).astype(jnp.float32)


def body(
    picture_tower_inputs,
    caption_tower_inputs,
    halfwidth_parameter_matrix,
    affinity_multiplier,
    affinity_offset,
    precise_parameter_copy,
    gradient_mean_estimate,
    gradient_variance_estimate,
):
    row_count, width = picture_tower_inputs.shape
    n_dp = lax.axis_size("dp")
    scale = affinity_multiplier[0]
    shift = affinity_offset[0]

    weights_img = gather_weights(halfwidth_parameter_matrix[:, :width])
    weights_txt = gather_weights(halfwidth_parameter_matrix[:, width:])
    unit_img, low_img, norm_img = project(picture_tower_inputs, weights_img)
    unit_txt, low_txt, norm_txt = project(caption_tower_inputs, weights_txt)

    y = bit_of("dp", 1)
    cuts = 2
    size = row_count // cuts
    own_across = jnp.where(y, low_img, low_txt)
    across = [swapped(own_across[:size], "dp", 1)]
    txt_behind, img_ahead = [], []
    for i in range(cuts):
        txt_behind.append(shifted(low_txt[i * size : (i + 1) * size], "dp", 2))
        img_ahead.append(shifted(low_img[i * size : (i + 1) * size], "dp", -2))
    onward = [(s, (s + (2 if s % 2 == 0 else -2)) % n_dp) for s in range(n_dp)]
    txt_beside, img_beside, last = [], [], []
    before = across[0]
    for i in range(cuts):
        txt_behind[i], before = lax.optimization_barrier((txt_behind[i], before))
        if i == 0:
            across[0] = before
        else:
            img_beside[i - 1] = before
        beside = swapped(txt_behind[i], "dp", 1)
        if i > 0:
            last.append(lax.ppermute(jnp.where(y, img_beside[i - 1], txt_beside[i - 1]), "dp", onward))
        img_ahead[i], beside = lax.optimization_barrier((img_ahead[i], beside))
        txt_beside.append(beside)
        before = swapped(img_ahead[i], "dp", 1)
        img_beside.append(before)
    rest, img_beside[-1] = lax.optimization_barrier((own_across[size:], img_beside[-1]))
    across.append(swapped(rest, "dp", 1))
    last.append(lax.ppermute(jnp.where(y, img_beside[-1], txt_beside[-1]), "dp", onward))

    def met(own, block, sign_label=-1.0):
        pair_weight = lax.optimization_barrier(weigh_pairs(own, block, scale, shift, sign_label))
        return pair_weight, jnp.dot(pair_weight, block, preferred_element_type=jnp.float32)

    diagonal = 2.0 * jnp.eye(row_count, dtype=jnp.float32) - 1.0
    pair_weight, grad_img = met(low_img, low_txt, diagonal)
    grad_txt = contract_rows(pair_weight, low_img)
    of_across = sum(met(own_across, v)[1] for v in across)
    grad_img = grad_img + jnp.where(y, of_across, 0.0)
    grad_txt = grad_txt + jnp.where(y, 0.0, of_across)
    for t, i in zip(txt_behind + txt_beside, img_ahead + img_beside):
        grad_img = grad_img + met(low_img, t)[1]
        grad_txt = grad_txt + met(low_txt, i)[1]
    own_last = jnp.where(y, low_txt, low_img)
    of_last = sum(met(own_last, v)[1] for v in last)
    grad_img = grad_img + jnp.where(y, 0.0, of_last)
    grad_txt = grad_txt + jnp.where(y, of_last, 0.0)
    img_tangent = tangent(norm_img, unit_img, grad_img)
    txt_tangent = tangent(norm_txt, unit_txt, grad_txt)

    owned = 2 * width // n_dp
    piece = width // 2
    pieces = weight_gradient(
        picture_tower_inputs, caption_tower_inputs, img_tangent, txt_tangent, n_dp, owned
    )
    shard_rows = width // lax.axis_size("fsdp")
    half = shard_rows // 2
    split = [p.reshape(2, 2, 2, half, piece) for p in pieces]

    new_parts = []
    for part in range(2):
        total = jnp.stack([s[:, :, part] for s in split]).reshape(2, 2, 2, 2, half, piece)
        total = reduce_half(total, 3, "fsdp", 1)
        if part == 0:
            total = reduce_half(total, 2, "fsdp", 2)
            total = reduce_half(total, 0, "dp", 1)
        else:
            total = reduce_half(total, 0, "dp", 1)
            total = reduce_half(total, 1, "fsdp", 2)
        total = reduce_half(total, 0, "dp", n_dp // 2)
        bit = n_dp // 4
        while bit > 1:
            size = total.shape[-1] // 2
            total = reduce_half(jnp.stack([total[:, :size], total[:, size:]]), 0, "dp", bit)
            bit //= 2
        rows = slice(part * half, (part + 1) * half)
        new_one = 0.9 * gradient_mean_estimate[rows] + 0.1 * total
        new_two = 0.95 * gradient_variance_estimate[rows] + 0.05 * total * total
        master = precise_parameter_copy[rows]
        new_master = master - 0.001 * (new_one / (jnp.sqrt(new_two) + 1e-08) + 0.1 * master)

        new_parts.append((new_master, new_one, new_two))
    new_master, new_one, new_two = (jnp.concatenate(both, axis=0) for both in zip(*new_parts))
    gathered = gather_columns(new_master.astype(jnp.bfloat16), n_dp)
    new_weights = gathered.transpose(1, 0, 2).reshape(shard_rows, 2 * width)
    return (img_tangent, txt_tangent, new_master, new_one, new_two, new_weights)


def solution(mesh):
    return jax.shard_map(
        body,
        mesh=mesh,
        in_specs=(
            P(("dp", "fsdp"), None),
            P(("dp", "fsdp"), None),
            P("fsdp", None),
            P(),
            P(),
            P("fsdp", "dp"),
            P("fsdp", "dp"),
            P("fsdp", "dp"),
        ),
        out_specs=(
            P(("dp", "fsdp"), None),
            P(("dp", "fsdp"), None),
            P("fsdp", "dp"),
            P("fsdp", "dp"),
            P("fsdp", "dp"),
            P("fsdp", None),
        ),
        check_vma=False,
    )
```

```python
import jax
import jax.numpy as jnp
from jax import lax
from jax.experimental import pallas as pl
from jax.experimental.pallas import tpu as pltpu
from jax.sharding import PartitionSpec as P

CYCLE = 4


def shifted(value, axis, steps):
    count = lax.axis_size(axis)
    pairs = [(source, (source + steps) % count) for source in range(count)]
    return lax.ppermute(value, axis, pairs)


def swapped(value, axis, bit):
    count = lax.axis_size(axis)
    return lax.ppermute(value, axis, [(source, source ^ bit) for source in range(count)])


def bit_of(axis, bit):
    return (lax.axis_index(axis) // bit) % 2 == 1


def ordered(mine, other, high):
    return jnp.where(high, other, mine), jnp.where(high, mine, other)


def project_kernel(rows_ref, weights_ref, unit_ref, low_ref, norm_ref):
    step = 128

    @pl.loop(0, rows_ref.shape[0] // step)
    def _(block):
        at = pl.ds(pl.multiple_of(block * step, step), step)
        projected = jnp.dot(
            rows_ref[at, :], weights_ref[...], preferred_element_type=jnp.float32
        )
        inv_norm = lax.rsqrt(jnp.sum(projected * projected, axis=-1, keepdims=True) + 1e-06)
        unit = projected * inv_norm
        unit_ref[at, :] = unit
        low_ref[at, :] = unit.astype(jnp.bfloat16)
        norm_ref[at, :] = inv_norm


def project(rows, weights):
    shape = (rows.shape[0], weights.shape[1])
    return pl.pallas_call(
        project_kernel,
        out_shape=(
            jax.ShapeDtypeStruct(shape, jnp.float32),
            jax.ShapeDtypeStruct(shape, jnp.bfloat16),
            jax.ShapeDtypeStruct((shape[0], 1), jnp.float32),
        ),
        in_specs=[pl.BlockSpec(memory_space=pltpu.VMEM)] * 2,
        out_specs=[pl.BlockSpec(memory_space=pltpu.VMEM)] * 3,
        compiler_params=pltpu.CompilerParams(vmem_limit_bytes=14 * 2**20),
    )(rows, weights)


def gather_kernel(own_ref, out_ref, z_send, z_recv, y_send, y_recv):
    n = out_ref.shape[0]
    steps = n // 2
    me = lax.axis_index("dp")
    after = lax.rem(me + 2, n)
    before = lax.rem(me + n - 2, n)
    beside = me + 1 - 2 * lax.rem(me, 2)
    barrier = pltpu.get_barrier_semaphore()
    for other in (after, before, beside):
        pl.semaphore_signal(
            barrier, inc=1, device_id={"dp": other}, device_id_type=pl.DeviceIdType.MESH
        )
    pl.semaphore_wait(barrier, 3)
    out_ref[me] = own_ref[...]
    along, across = [], []
    for step in range(steps):
        block = lax.rem(me - 2 * step + 2 * n, n)
        if step > 0:
            along[step - 1].wait_recv()
        for copies, target, sends, receives in (
            (along, after, z_send, z_recv),
            (across, beside, y_send, y_recv),
        ):
            if copies is along and step == steps - 1:
                continue
            copy = pltpu.make_async_remote_copy(
                src_ref=out_ref.at[block],
                dst_ref=out_ref.at[block],
                send_sem=sends.at[step],
                recv_sem=receives.at[step],
                device_id={"dp": target},
                device_id_type=pl.DeviceIdType.MESH,
            )
            copy.start()
            copies.append(copy)
    for copy in along:
        copy.wait_send()
    for copy in across:
        copy.wait()


def gather_columns(own, n_dp):
    return pl.pallas_call(
        gather_kernel,
        out_shape=jax.ShapeDtypeStruct((n_dp,) + own.shape, own.dtype),
        in_specs=[pl.BlockSpec(memory_space=pltpu.VMEM)],
        out_specs=pl.BlockSpec(memory_space=pltpu.VMEM),
        scratch_shapes=[pltpu.SemaphoreType.DMA((n_dp // 2,))] * 4,
        compiler_params=pltpu.CompilerParams(
            collective_id=0, has_side_effects=True, vmem_limit_bytes=6 * 2**20
        ),
    )(own)


def contract_rows(left, right):
    return lax.dot_general(
        left, right, (((0,), (0,)), ((), ())), preferred_element_type=jnp.float32
    )


def weigh_pairs(left, right, scale, shift, sign_label):
    logits = (
        scale
        * lax.dot_general(
            left, right, (((1,), (1,)), ((), ())), preferred_element_type=jnp.float32
        )
        + shift
    )
    return (-sign_label * jax.nn.sigmoid(-sign_label * logits) * scale).astype(jnp.bfloat16)


def gather_weights(shard):
    rows = shard.shape[0]
    half = rows // 2
    y = bit_of("dp", 1)
    x = bit_of("fsdp", 2)
    c = bit_of("fsdp", 1)
    mine = jnp.where(y, shard[half:], shard[:half])
    got = swapped(mine, "fsdp", 2)
    rest = swapped(got, "dp", 1)
    low, high = ordered(got, rest, y)
    remote = jnp.concatenate([low, high], axis=0)
    own_core = swapped(shard, "fsdp", 1)
    remote_core = swapped(remote, "fsdp", 1)
    own_pair = jnp.concatenate(ordered(shard, own_core, c), axis=0)
    remote_pair = jnp.concatenate(ordered(remote, remote_core, c), axis=0)
    return jnp.concatenate(ordered(own_pair, remote_pair, x), axis=0)


def tangent(inv_norm, unit, grad):
    return (inv_norm * (grad - unit * jnp.sum(unit * grad, axis=1, keepdims=True))).astype(
        jnp.bfloat16
    )


def gradient_kernel(img_ref, txt_ref, img_tan_ref, txt_tan_ref, order_ref, out_ref, columns_ref):
    row_count, width = img_ref.shape
    piece = out_ref.shape[-1]
    padded = columns_ref.shape[-1] // 2
    step = 384 if width % 384 == 0 else 128
    for tower, (features, rows) in enumerate(((img_ref, img_tan_ref), (txt_ref, txt_tan_ref))):
        for start in range(0, row_count, 256):
            chunk = slice(start, start + 256)
            columns_ref[chunk, :] = jnp.dot(
                rows[chunk, :], order_ref[...], preferred_element_type=jnp.float32
            ).astype(jnp.bfloat16)

        @pl.loop(0, width // step)
        def _(block):
            at = pl.multiple_of(block * step, step)
            left = features[:, pl.ds(at, step)]
            for y in range(2):
                right = columns_ref[:, y * padded : y * padded + piece]
                out_ref[y, tower, pl.ds(at, step), :] = contract_rows(left, right).astype(
                    jnp.bfloat16
                )


def weight_gradient(img, txt, img_tangent, txt_tangent, n_dp, owned):
    row_count, width = img.shape
    piece = width // 2
    padded = -(-piece // 128) * 128
    source = jnp.arange(width)
    block = source // owned
    target = (block % 2) * padded + (block // 2) * owned + source % owned
    order = (target[:, None] == jnp.arange(2 * padded)[None, :]).astype(jnp.bfloat16)
    out = pl.pallas_call(
        gradient_kernel,
        out_shape=jax.ShapeDtypeStruct((2, 2, width, piece), jnp.bfloat16),
        in_specs=[pl.BlockSpec(memory_space=pltpu.VMEM)] * 5,
        out_specs=pl.BlockSpec(memory_space=pltpu.VMEM),
        scratch_shapes=[pltpu.VMEM((row_count, 2 * padded), jnp.bfloat16)],
        compiler_params=pltpu.CompilerParams(vmem_limit_bytes=22 * 2**20),
    )(img, txt, img_tangent, txt_tangent, order)
    return [out[y, tower] for y in range(2) for tower in range(2)]


def reduce_half(value, dim, axis, bit):
    high = bit_of(axis, bit)
    low_half = lax.index_in_dim(value, 0, dim, keepdims=False)
    high_half = lax.index_in_dim(value, 1, dim, keepdims=False)
    send = jnp.where(high, low_half, high_half).astype(jnp.bfloat16)
    keep = jnp.where(high, high_half, low_half).astype(jnp.float32)
    return keep + swapped(send, axis, bit).astype(jnp.float32)


def body(
    picture_tower_inputs,
    caption_tower_inputs,
    halfwidth_parameter_matrix,
    affinity_multiplier,
    affinity_offset,
    precise_parameter_copy,
    gradient_mean_estimate,
    gradient_variance_estimate,
):
    row_count, width = picture_tower_inputs.shape
    n_dp = lax.axis_size("dp")
    scale = affinity_multiplier[0]
    shift = affinity_offset[0]

    weights_txt = gather_weights(halfwidth_parameter_matrix[:, width:])
    weights_img = gather_weights(halfwidth_parameter_matrix[:, :width])
    unit_txt, low_txt, norm_txt = project(caption_tower_inputs, weights_txt)
    weights_img, unit_txt = lax.optimization_barrier((weights_img, unit_txt))
    unit_img, low_img, norm_img = project(picture_tower_inputs, weights_img)

    y = bit_of("dp", 1)
    cuts = 2
    size = row_count // cuts
    own_across = jnp.where(y, low_img, low_txt)
    across = [swapped(own_across[:size], "dp", 1)]
    txt_behind, img_ahead = [], []
    for i in range(cuts):
        part_txt, part_img = (v[i * size : (i + 1) * size] for v in (low_txt, low_img))
        if i > 0:
            part_txt, txt_behind[-1] = lax.optimization_barrier((part_txt, txt_behind[-1]))
            part_img, img_ahead[-1] = lax.optimization_barrier((part_img, img_ahead[-1]))
        txt_behind.append(shifted(part_txt, "dp", 2))
        img_ahead.append(shifted(part_img, "dp", -2))
    onward = [(s, (s + (2 if s % 2 == 0 else -2)) % n_dp) for s in range(n_dp)]
    txt_beside, img_beside, last = [], [], []
    before = across[0]
    for i in range(cuts):
        txt_behind[i], before = lax.optimization_barrier((txt_behind[i], before))
        if i == 0:
            across[0] = before
        else:
            img_beside[i - 1] = before
        beside = swapped(txt_behind[i], "dp", 1)
        if i > 0:
            last.append(lax.ppermute(jnp.where(y, img_beside[i - 1], txt_beside[i - 1]), "dp", onward))
        img_ahead[i], beside = lax.optimization_barrier((img_ahead[i], beside))
        txt_beside.append(beside)
        before = swapped(img_ahead[i], "dp", 1)
        img_beside.append(before)
    rest, img_beside[-1] = lax.optimization_barrier((own_across[size:], img_beside[-1]))
    across.append(swapped(rest, "dp", 1))
    last.append(lax.ppermute(jnp.where(y, img_beside[-1], txt_beside[-1]), "dp", onward))

    def met(own, block, sign_label=-1.0):
        pair_weight = lax.optimization_barrier(weigh_pairs(own, block, scale, shift, sign_label))
        return pair_weight, jnp.dot(pair_weight, block, preferred_element_type=jnp.float32)

    diagonal = 2.0 * jnp.eye(row_count, dtype=jnp.float32) - 1.0
    pair_weight, grad_img = met(low_img, low_txt, diagonal)
    grad_txt = contract_rows(pair_weight, low_img)
    of_across = sum(met(own_across, v)[1] for v in across)
    grad_img = grad_img + jnp.where(y, of_across, 0.0)
    grad_txt = grad_txt + jnp.where(y, 0.0, of_across)
    for t, i in zip(txt_behind + txt_beside, img_ahead + img_beside):
        grad_img = grad_img + met(low_img, t)[1]
        grad_txt = grad_txt + met(low_txt, i)[1]
    own_last = jnp.where(y, low_txt, low_img)
    of_last = sum(met(own_last, v)[1] for v in last)
    grad_img = grad_img + jnp.where(y, 0.0, of_last)
    grad_txt = grad_txt + jnp.where(y, of_last, 0.0)
    img_tangent = tangent(norm_img, unit_img, grad_img)
    txt_tangent = tangent(norm_txt, unit_txt, grad_txt)

    owned = 2 * width // n_dp
    piece = width // 2
    pieces = weight_gradient(
        picture_tower_inputs, caption_tower_inputs, img_tangent, txt_tangent, n_dp, owned
    )
    shard_rows = width // lax.axis_size("fsdp")
    half = shard_rows // 2
    split = [p.reshape(2, 2, 2, half, piece) for p in pieces]

    new_parts = []
    for part in range(2):
        total = jnp.stack([s[:, :, part] for s in split]).reshape(2, 2, 2, 2, half, piece)
        total = reduce_half(total, 3, "fsdp", 1)
        if part == 0:
            total = reduce_half(total, 2, "fsdp", 2)
            total = reduce_half(total, 0, "dp", 1)
        else:
            total = reduce_half(total, 0, "dp", 1)
            total = reduce_half(total, 1, "fsdp", 2)
        total = reduce_half(total, 0, "dp", n_dp // 2)
        bit = n_dp // 4
        while bit > 1:
            size = total.shape[-1] // 2
            total = reduce_half(jnp.stack([total[:, :size], total[:, size:]]), 0, "dp", bit)
            bit //= 2
        rows = slice(part * half, (part + 1) * half)
        new_one = 0.9 * gradient_mean_estimate[rows] + 0.1 * total
        new_two = 0.95 * gradient_variance_estimate[rows] + 0.05 * total * total
        master = precise_parameter_copy[rows]
        new_master = master - 0.001 * (new_one / (jnp.sqrt(new_two) + 1e-08) + 0.1 * master)

        new_parts.append((new_master, new_one, new_two))
    new_master, new_one, new_two = (jnp.concatenate(both, axis=0) for both in zip(*new_parts))
    gathered = gather_columns(new_master.astype(jnp.bfloat16), n_dp)
    new_weights = gathered.transpose(1, 0, 2).reshape(shard_rows, 2 * width)
    return (img_tangent, txt_tangent, new_master, new_one, new_two, new_weights)


def solution(mesh):
    return jax.shard_map(
        body,
        mesh=mesh,
        in_specs=(
            P(("dp", "fsdp"), None),
            P(("dp", "fsdp"), None),
            P("fsdp", None),
            P(),
            P(),
            P("fsdp", "dp"),
            P("fsdp", "dp"),
            P("fsdp", "dp"),
        ),
        out_specs=(
            P(("dp", "fsdp"), None),
            P(("dp", "fsdp"), None),
            P("fsdp", "dp"),
            P("fsdp", "dp"),
            P("fsdp", "dp"),
            P("fsdp", None),
        ),
        check_vma=False,
    )
```

```python
import jax
import jax.numpy as jnp
from jax import lax
from jax.experimental import pallas as pl
from jax.experimental.pallas import tpu as pltpu
from jax.sharding import PartitionSpec as P

CYCLE = 4


def shifted(value, axis, steps):
    count = lax.axis_size(axis)
    pairs = [(source, (source + steps) % count) for source in range(count)]
    return lax.ppermute(value, axis, pairs)


def swapped(value, axis, bit):
    count = lax.axis_size(axis)
    return lax.ppermute(value, axis, [(source, source ^ bit) for source in range(count)])


def bit_of(axis, bit):
    return (lax.axis_index(axis) // bit) % 2 == 1


def ordered(mine, other, high):
    return jnp.where(high, other, mine), jnp.where(high, mine, other)


def project_kernel(rows_ref, weights_ref, unit_ref, low_ref, norm_ref):
    step = 128

    @pl.loop(0, rows_ref.shape[0] // step)
    def _(block):
        at = pl.ds(pl.multiple_of(block * step, step), step)
        projected = jnp.dot(
            rows_ref[at, :], weights_ref[...], preferred_element_type=jnp.float32
        )
        inv_norm = lax.rsqrt(jnp.sum(projected * projected, axis=-1, keepdims=True) + 1e-06)
        unit = projected * inv_norm
        unit_ref[at, :] = unit
        low_ref[at, :] = unit.astype(jnp.bfloat16)
        norm_ref[at, :] = inv_norm


def project(rows, weights):
    shape = (rows.shape[0], weights.shape[1])
    return pl.pallas_call(
        project_kernel,
        out_shape=(
            jax.ShapeDtypeStruct(shape, jnp.float32),
            jax.ShapeDtypeStruct(shape, jnp.bfloat16),
            jax.ShapeDtypeStruct((shape[0], 1), jnp.float32),
        ),
        in_specs=[pl.BlockSpec(memory_space=pltpu.VMEM)] * 2,
        out_specs=[pl.BlockSpec(memory_space=pltpu.VMEM)] * 3,
        compiler_params=pltpu.CompilerParams(vmem_limit_bytes=32 * 2**20),
    )(rows, weights)


def gather_kernel(own_ref, out_ref, z_send, z_recv, y_send, y_recv):
    n = out_ref.shape[0]
    steps = n // 2
    me = lax.axis_index("dp")
    after = lax.rem(me + 2, n)
    before = lax.rem(me + n - 2, n)
    beside = me + 1 - 2 * lax.rem(me, 2)
    barrier = pltpu.get_barrier_semaphore()
    for other in (after, before, beside):
        pl.semaphore_signal(
            barrier, inc=1, device_id={"dp": other}, device_id_type=pl.DeviceIdType.MESH
        )
    pl.semaphore_wait(barrier, 3)
    out_ref[me] = own_ref[...]
    along, across = [], []
    for step in range(steps):
        block = lax.rem(me - 2 * step + 2 * n, n)
        if step > 0:
            along[step - 1].wait_recv()
        for copies, target, sends, receives in (
            (along, after, z_send, z_recv),
            (across, beside, y_send, y_recv),
        ):
            if copies is along and step == steps - 1:
                continue
            copy = pltpu.make_async_remote_copy(
                src_ref=out_ref.at[block],
                dst_ref=out_ref.at[block],
                send_sem=sends.at[step],
                recv_sem=receives.at[step],
                device_id={"dp": target},
                device_id_type=pl.DeviceIdType.MESH,
            )
            copy.start()
            copies.append(copy)
    for copy in along:
        copy.wait_send()
    for copy in across:
        copy.wait()


def gather_columns(own, n_dp):
    return pl.pallas_call(
        gather_kernel,
        out_shape=jax.ShapeDtypeStruct((n_dp,) + own.shape, own.dtype),
        in_specs=[pl.BlockSpec(memory_space=pltpu.VMEM)],
        out_specs=pl.BlockSpec(memory_space=pltpu.VMEM),
        scratch_shapes=[pltpu.SemaphoreType.DMA((n_dp // 2,))] * 4,
        compiler_params=pltpu.CompilerParams(
            collective_id=0, has_side_effects=True, vmem_limit_bytes=32 * 2**20
        ),
    )(own)


def contract_rows(left, right):
    return lax.dot_general(
        left, right, (((0,), (0,)), ((), ())), preferred_element_type=jnp.float32
    )


def weigh_pairs(left, right, scale, shift, sign_label):
    logits = (
        scale
        * lax.dot_general(
            left, right, (((1,), (1,)), ((), ())), preferred_element_type=jnp.float32
        )
        + shift
    )
    return (-sign_label * jax.nn.sigmoid(-sign_label * logits) * scale).astype(jnp.bfloat16)


def gather_weights(shard):
    rows = shard.shape[0]
    half = rows // 2
    y = bit_of("dp", 1)
    x = bit_of("fsdp", 2)
    c = bit_of("fsdp", 1)
    mine = jnp.where(y, shard[half:], shard[:half])
    got = swapped(mine, "fsdp", 2)
    rest = swapped(got, "dp", 1)
    low, high = ordered(got, rest, y)
    remote = jnp.concatenate([low, high], axis=0)
    own_core = swapped(shard, "fsdp", 1)
    remote_core = swapped(remote, "fsdp", 1)
    own_pair = jnp.concatenate(ordered(shard, own_core, c), axis=0)
    remote_pair = jnp.concatenate(ordered(remote, remote_core, c), axis=0)
    return jnp.concatenate(ordered(own_pair, remote_pair, x), axis=0)


def tangent(inv_norm, unit, grad):
    return (inv_norm * (grad - unit * jnp.sum(unit * grad, axis=1, keepdims=True))).astype(
        jnp.bfloat16
    )


def gradient_kernel(img_ref, txt_ref, img_tan_ref, txt_tan_ref, order_ref, out_ref, columns_ref):
    row_count, width = img_ref.shape
    piece = out_ref.shape[-1]
    padded = columns_ref.shape[-1] // 2
    step = 384 if width % 384 == 0 else 128
    for tower, (features, rows) in enumerate(((img_ref, img_tan_ref), (txt_ref, txt_tan_ref))):
        for start in range(0, row_count, 256):
            chunk = slice(start, start + 256)
            columns_ref[chunk, :] = jnp.dot(
                rows[chunk, :], order_ref[...], preferred_element_type=jnp.float32
            ).astype(jnp.bfloat16)

        @pl.loop(0, width // step)
        def _(block):
            at = pl.multiple_of(block * step, step)
            left = features[:, pl.ds(at, step)]
            for y in range(2):
                right = columns_ref[:, y * padded : y * padded + piece]
                out_ref[y, tower, pl.ds(at, step), :] = contract_rows(left, right).astype(
                    jnp.bfloat16
                )


def weight_gradient(img, txt, img_tangent, txt_tangent, n_dp, owned):
    row_count, width = img.shape
    piece = width // 2
    padded = -(-piece // 128) * 128
    source = jnp.arange(width)
    block = source // owned
    target = (block % 2) * padded + (block // 2) * owned + source % owned
    order = (target[:, None] == jnp.arange(2 * padded)[None, :]).astype(jnp.bfloat16)
    out = pl.pallas_call(
        gradient_kernel,
        out_shape=jax.ShapeDtypeStruct((2, 2, width, piece), jnp.bfloat16),
        in_specs=[pl.BlockSpec(memory_space=pltpu.VMEM)] * 5,
        out_specs=pl.BlockSpec(memory_space=pltpu.VMEM),
        scratch_shapes=[pltpu.VMEM((row_count, 2 * padded), jnp.bfloat16)],
        compiler_params=pltpu.CompilerParams(vmem_limit_bytes=32 * 2**20),
    )(img, txt, img_tangent, txt_tangent, order)
    return [out[y, tower] for y in range(2) for tower in range(2)]


def reduce_half(value, dim, axis, bit):
    high = bit_of(axis, bit)
    low_half = lax.index_in_dim(value, 0, dim, keepdims=False)
    high_half = lax.index_in_dim(value, 1, dim, keepdims=False)
    send = jnp.where(high, low_half, high_half).astype(jnp.bfloat16)
    keep = jnp.where(high, high_half, low_half).astype(jnp.float32)
    return keep + swapped(send, axis, bit).astype(jnp.float32)


def body(
    picture_tower_inputs,
    caption_tower_inputs,
    halfwidth_parameter_matrix,
    affinity_multiplier,
    affinity_offset,
    precise_parameter_copy,
    gradient_mean_estimate,
    gradient_variance_estimate,
):
    row_count, width = picture_tower_inputs.shape
    n_dp = lax.axis_size("dp")
    scale = affinity_multiplier[0]
    shift = affinity_offset[0]

    weights_img = gather_weights(halfwidth_parameter_matrix[:, :width])
    weights_txt = gather_weights(halfwidth_parameter_matrix[:, width:])
    unit_img, low_img, norm_img = project(picture_tower_inputs, weights_img)
    unit_txt, low_txt, norm_txt = project(caption_tower_inputs, weights_txt)

    y = bit_of("dp", 1)
    cuts = 2
    size = row_count // cuts
    own_across = jnp.where(y, low_img, low_txt)
    across = [swapped(own_across[:size], "dp", 1)]
    txt_behind, img_ahead = [], []
    for i in range(cuts):
        part_txt, part_img = (v[i * size : (i + 1) * size] for v in (low_txt, low_img))
        if i > 0:
            part_txt, txt_behind[-1] = lax.optimization_barrier((part_txt, txt_behind[-1]))
            part_img, img_ahead[-1] = lax.optimization_barrier((part_img, img_ahead[-1]))
        txt_behind.append(shifted(part_txt, "dp", 2))
        img_ahead.append(shifted(part_img, "dp", -2))
    onward = [(s, (s + (2 if s % 2 == 0 else -2)) % n_dp) for s in range(n_dp)]
    txt_beside, img_beside, last = [], [], []
    before = across[0]
    for i in range(cuts):
        txt_behind[i], before = lax.optimization_barrier((txt_behind[i], before))
        if i == 0:
            across[0] = before
        else:
            img_beside[i - 1] = before
        beside = swapped(txt_behind[i], "dp", 1)
        if i > 0:
            last.append(lax.ppermute(jnp.where(y, img_beside[i - 1], txt_beside[i - 1]), "dp", onward))
        img_ahead[i], beside = lax.optimization_barrier((img_ahead[i], beside))
        txt_beside.append(beside)
        before = swapped(img_ahead[i], "dp", 1)
        img_beside.append(before)
    rest, img_beside[-1] = lax.optimization_barrier((own_across[size:], img_beside[-1]))
    across.append(swapped(rest, "dp", 1))
    last.append(lax.ppermute(jnp.where(y, img_beside[-1], txt_beside[-1]), "dp", onward))

    def met(own, block, sign_label=-1.0):
        pair_weight = lax.optimization_barrier(weigh_pairs(own, block, scale, shift, sign_label))
        return pair_weight, jnp.dot(pair_weight, block, preferred_element_type=jnp.float32)

    diagonal = 2.0 * jnp.eye(row_count, dtype=jnp.float32) - 1.0
    pair_weight, grad_img = met(low_img, low_txt, diagonal)
    grad_txt = contract_rows(pair_weight, low_img)
    of_across = sum(met(own_across, v)[1] for v in across)
    grad_img = grad_img + jnp.where(y, of_across, 0.0)
    grad_txt = grad_txt + jnp.where(y, 0.0, of_across)
    for t, i in zip(txt_behind + txt_beside, img_ahead + img_beside):
        grad_img = grad_img + met(low_img, t)[1]
        grad_txt = grad_txt + met(low_txt, i)[1]
    own_last = jnp.where(y, low_txt, low_img)
    of_last = sum(met(own_last, v)[1] for v in last)
    grad_img = grad_img + jnp.where(y, 0.0, of_last)
    grad_txt = grad_txt + jnp.where(y, of_last, 0.0)
    img_tangent = tangent(norm_img, unit_img, grad_img)
    txt_tangent = tangent(norm_txt, unit_txt, grad_txt)

    owned = 2 * width // n_dp
    piece = width // 2
    pieces = weight_gradient(
        picture_tower_inputs, caption_tower_inputs, img_tangent, txt_tangent, n_dp, owned
    )
    shard_rows = width // lax.axis_size("fsdp")
    half = shard_rows // 2
    split = [p.reshape(2, 2, 2, half, piece) for p in pieces]

    new_parts = []
    for part in range(2):
        total = jnp.stack([s[:, :, part] for s in split]).reshape(2, 2, 2, 2, half, piece)
        total = reduce_half(total, 3, "fsdp", 1)
        if part == 0:
            total = reduce_half(total, 2, "fsdp", 2)
            total = reduce_half(total, 0, "dp", 1)
        else:
            total = reduce_half(total, 0, "dp", 1)
            total = reduce_half(total, 1, "fsdp", 2)
        total = reduce_half(total, 0, "dp", n_dp // 2)
        bit = n_dp // 4
        while bit > 1:
            size = total.shape[-1] // 2
            total = reduce_half(jnp.stack([total[:, :size], total[:, size:]]), 0, "dp", bit)
            bit //= 2
        rows = slice(part * half, (part + 1) * half)
        new_one = 0.9 * gradient_mean_estimate[rows] + 0.1 * total
        new_two = 0.95 * gradient_variance_estimate[rows] + 0.05 * total * total
        master = precise_parameter_copy[rows]
        new_master = master - 0.001 * (new_one / (jnp.sqrt(new_two) + 1e-08) + 0.1 * master)

        new_parts.append((new_master, new_one, new_two))
    new_master, new_one, new_two = (jnp.concatenate(both, axis=0) for both in zip(*new_parts))
    gathered = gather_columns(new_master.astype(jnp.bfloat16), n_dp)
    new_weights = gathered.transpose(1, 0, 2).reshape(shard_rows, 2 * width)
    return (img_tangent, txt_tangent, new_master, new_one, new_two, new_weights)


def solution(mesh):
    return jax.shard_map(
        body,
        mesh=mesh,
        in_specs=(
            P(("dp", "fsdp"), None),
            P(("dp", "fsdp"), None),
            P("fsdp", None),
            P(),
            P(),
            P("fsdp", "dp"),
            P("fsdp", "dp"),
            P("fsdp", "dp"),
        ),
        out_specs=(
            P(("dp", "fsdp"), None),
            P(("dp", "fsdp"), None),
            P("fsdp", "dp"),
            P("fsdp", "dp"),
            P("fsdp", "dp"),
            P("fsdp", None),
        ),
        check_vma=False,
    )
```
